1024 devices in a mesh: face: 16 (over x, core), blk: 64 (over z, y).
Axes of the slice: x: 8, y: 8, z: 8, core: 2. Of those that a mesh axis runs over, the one named last changes fastest.
Arguments:
- tracer: float32 [512, 2048, 128], P('face', 'blk'), may hold values from -6 to 6
- wind_x: bfloat16 [512, 2048, 128], P('face', 'blk'), may hold values from -0.25 to 0.25
- wind_y: bfloat16 [512, 2048, 128], P('face', 'blk'), may hold values from -0.25 to 0.25
- cell_area: float32 [512, 2048], P('face', 'blk'), may hold values from 0.5 to 2
- forcing: bfloat16 [512, 2048, 384], P('face', 'blk'), may hold values from -6 to 6
- group_map: int32 [512, 2048], P('face', 'blk'), may hold values from -1 to 1023, as said below
- w_in: bfloat16 [64, 512, 512], P('blk'), may hold values from -0.375 to 0.375
- w_hidden: bfloat16 [64, 4, 512, 512], P('blk'), may hold values from -0.375 to 0.375
- w_out: bfloat16 [64, 512, 256], P('blk'), may hold values from -0.25 to 0.25
Outputs:
- advected: float32 [512, 2048, 128], P('face', 'blk')
- tendencies: bfloat16 [512, 2048, 256], P('face', 'blk')
The draws below stay inside these ranges and needn't reach their ends.
Inputs may be any that keep to these rules, and one draw needn't show every extreme that they name: A column with group_map -1 is not called. Otherwise the value is d * 16 + p: the column goes to physics group d, held by blk index d with the same face index, at place p. The places that one device gives one group are 0 to n-1 without gaps, with n at most 16. Every group receives exactly 384 columns, from 25 devices of its blk group: all but two of them send exactly 16, the other two send amounts that add to 16.
All inputs are finite; a program needn't handle non-finite values.
Results may differ from the reference program's by a relative error of at most 0.0077.
Values may be sent and summed in bfloat16 or wider, within the bound.
No kernel may reach another device: no remote copies, remote signals or barrier semaphores. Data moves between devices by JAX's collectives and lax.ppermute only.
A program may use at most 32 MiB of HBM per device.

```python
import math
import jax
import jax.numpy as jnp
from jax import lax

CX = 32
CY = 32
LEV = 128
HID = 512
L_HID = 4
NX = 512
NY = 2048
CAP = 16
SOURCES = 24
GROUP_ROWS = 384
FIN = 512
FOUT = 256
N_FACE = 16
N_BLK = 64


def draw_group_map(key, part):
    key = jax.random.fold_in(key, 11)
    subkeys = jax.random.split(key, 4)
    columns = CX * CY
    source_ids = jnp.arange(N_BLK, dtype=jnp.int32)
    leaning = jax.random.randint(subkeys[0], (N_FACE, 1, N_BLK), 0, 3 * N_BLK)
    jitter = jax.random.randint(subkeys[1], (N_FACE, N_BLK, N_BLK), 0, N_BLK)
    scores = (leaning + jitter) * N_BLK + source_ids
    chosen = lax.top_k(scores, SOURCES + 1)[1].astype(jnp.int32)
    split_part = jax.random.randint(subkeys[2], (N_FACE, N_BLK, 1), 1, CAP).astype(jnp.int32)
    amounts = jnp.concatenate([jnp.full((N_FACE, N_BLK, SOURCES - 1), CAP, jnp.int32), split_part, CAP - split_part], axis=2)
    sent_counts = jnp.sum(jnp.where(chosen[..., None] == source_ids, amounts[..., None], 0), axis=2)
    sent_counts = jnp.transpose(sent_counts, (0, 2, 1))
    run_ends = jnp.cumsum(sent_counts, axis=2)
    run_starts = run_ends - sent_counts
    ranking = jnp.argsort(jax.random.randint(subkeys[3], (N_FACE, N_BLK, columns), 0, columns) * columns + jnp.arange(columns, dtype=jnp.int32), axis=2).astype(jnp.int32)
    span_index = jnp.sum((run_ends[:, :, None, :] <= ranking[..., None]).astype(jnp.int32), axis=3)
    is_live = ranking < run_ends[:, :, -1:]
    clipped = jnp.minimum(span_index, N_BLK - 1)
    begin_at = jnp.take_along_axis(run_starts, clipped, axis=2)
    mapped = jnp.where(is_live, clipped * CAP + ranking - begin_at, -1)
    tiled_map = mapped.reshape(N_FACE, N_BLK, CX, CY).transpose(0, 2, 1, 3).reshape(N_FACE * CX, N_BLK * CY)
    return tiled_map.astype(jnp.int32)


def block_scale(rng, extent, shards, low, largest):
    factor_of, own = 1.0, jax.random.fold_in(rng, 6)
    for position, blocks in shards:
        steps = jnp.exp(jax.random.uniform(jax.random.fold_in(own, position), (blocks,), jnp.float32, low / len(shards), largest / len(shards)))
        factor_of = factor_of * jnp.repeat(steps, extent[position] // blocks).reshape([-1 if axis == position else 1 for axis in range(len(extent))])
    return factor_of


def bell_draw(rng, extent, scale, reach, cuts=(), kind=jnp.bfloat16):
    factor_of = block_scale(rng, extent, cuts, -0.22, 0.18) if cuts else 1.0
    result = jax.random.normal(rng, extent, jnp.float32) * scale * factor_of
    return jnp.minimum(jnp.maximum(result, -reach), reach).astype(kind)


def setup_inputs(seed: int = 0) -> dict:
    seeds = jax.random.split(jax.random.key(seed), 10)
    tracer = bell_draw(seeds[0], (NX, NY, LEV), 1.0, 6.0, ((0, 16), (1, 64)), jnp.float32)
    wind_x = jnp.clip(jax.random.uniform(seeds[1], (NX, NY, LEV), jnp.float32, -0.25, 0.25) * block_scale(seeds[1], (NX, NY, LEV), ((0, 16), (1, 64)), -0.4, 0.0), -0.25, 0.25).astype(jnp.bfloat16)
    wind_y = jnp.clip(jax.random.uniform(seeds[2], (NX, NY, LEV), jnp.float32, -0.25, 0.25) * block_scale(seeds[2], (NX, NY, LEV), ((0, 16), (1, 64)), -0.4, 0.0), -0.25, 0.25).astype(jnp.bfloat16)
    cell_area = jnp.clip(jnp.exp(math.log(2.0) - 1.3862944 * jax.random.uniform(seeds[3], (NX, NY), jnp.float32) ** block_scale(seeds[3], (NX, NY), ((0, 16), (1, 64)), -0.2, 0.2)), 0.5, 2.0)
    forcing = bell_draw(seeds[4], (NX, NY, 3 * LEV), 1.0, 6.0, ((0, 16), (1, 64)))
    group_map = draw_group_map(jax.random.fold_in(seeds[9], 71), 0)
    w_in = bell_draw(seeds[6], (N_BLK, FIN, HID), (FIN // 2) ** -0.5, 0.375, ((0, 64),))
    w_hidden = bell_draw(seeds[7], (N_BLK, L_HID, HID, HID), (HID // 2) ** -0.5, 0.375, ((0, 64),))
    w_out = bell_draw(seeds[8], (N_BLK, HID, FOUT), HID ** -0.5, 0.25, ((0, 64),))
    return {"tracer": tracer, "wind_x": wind_x, "wind_y": wind_y, "cell_area": cell_area, "forcing": forcing, "group_map": group_map, "w_in": w_in, "w_hidden": w_hidden, "w_out": w_out}


def leaky_relu(values):
    return jnp.maximum(values, 0.15 * values)


def column_net(in_rows, w_in, w_hidden, w_out):
    hidden = leaky_relu(jnp.dot(in_rows, w_in, preferred_element_type=jnp.float32)).astype(jnp.bfloat16)
    for layer_index in range(L_HID):
        hidden = leaky_relu(jnp.dot(hidden, w_hidden[layer_index], preferred_element_type=jnp.float32)).astype(jnp.bfloat16)
    return jnp.dot(hidden, w_out, preferred_element_type=jnp.float32).astype(jnp.bfloat16)


def reference(tracer, wind_x, wind_y, cell_area, forcing, group_map, w_in, w_hidden, w_out):
    speed_x = wind_x.astype(jnp.float32)
    speed_y = wind_y.astype(jnp.float32)
    flux_x = jnp.maximum(speed_x, 0.0) * tracer + jnp.minimum(speed_x, 0.0) * jnp.roll(tracer, -1, axis=0)
    flux_y = jnp.maximum(speed_y, 0.0) * tracer + jnp.minimum(speed_y, 0.0) * jnp.roll(tracer, -1, axis=1)
    spread = (flux_x - jnp.roll(flux_x, 1, axis=0)) + (flux_y - jnp.roll(flux_y, 1, axis=1))
    advected = tracer - spread / cell_area[:, :, None]
    faces_adv = advected.reshape(N_FACE, CX, NY, LEV)
    faces_force = forcing.reshape(N_FACE, CX, NY, 3 * LEV)
    faces_map = group_map.reshape(N_FACE, CX * NY)
    group_ids = jnp.arange(N_BLK, dtype=jnp.int32)

    def one_face(inputs):
        face_adv, face_force, face_map = inputs
        features = jnp.concatenate([face_adv.astype(jnp.bfloat16), face_force], axis=2).reshape(CX * NY, FIN)
        owner = jnp.where(face_map >= 0, face_map // CAP, -1).astype(jnp.int32)

        def one_group(group_args):
            group_id, group_in, group_hidden, group_out = group_args
            picked = jnp.nonzero(owner == group_id, size=GROUP_ROWS)[0].astype(jnp.int32)
            return picked, column_net(features[picked], group_in, group_hidden, group_out)

        picked_all, outputs = lax.map(one_group, (group_ids, w_in, w_hidden, w_out))
        return jnp.zeros((CX * NY, FOUT), jnp.bfloat16).at[picked_all.reshape(-1)].set(outputs.reshape(-1, FOUT))

    tendencies = lax.map(one_face, (faces_adv, faces_force, faces_map))
    return advected, tendencies.reshape(NX, NY, FOUT)
```

```python
import jax
import jax.numpy as jnp
from jax import lax
from jax.experimental import pallas as pl
from jax.experimental.pallas import tpu as pltpu
from jax.sharding import PartitionSpec as P

SLOPE = 0.15
VMEM = pl.BlockSpec(memory_space=pltpu.VMEM)


def call(kernel, outs, operands, name, flops=0, touched=0, scratch=(), limit=48 << 20):
    return pl.pallas_call(
        kernel,
        out_shape=outs,
        in_specs=[VMEM] * len(operands),
        out_specs=jax.tree.map(lambda _: VMEM, outs),
        scratch_shapes=list(scratch),
        compiler_params=pltpu.CompilerParams(vmem_limit_bytes=limit),
        cost_estimate=pl.CostEstimate(flops=flops, bytes_accessed=touched, transcendentals=0),
        name=name,
    )(*operands)


def edges_kernel(tracer, wind_x, wind_y, last_x, first_x, last_y, first_y):
    cells_x, cells_y, _ = tracer.shape
    last_x[0] = tracer[cells_x - 1]
    last_x[1] = wind_x[cells_x - 1].astype(jnp.float32)
    first_x[...] = tracer[0]
    last_y[0] = tracer[:, cells_y - 1, :]
    last_y[1] = wind_y[...].astype(jnp.float32)[:, cells_y - 1, :]
    first_y[...] = tracer[:, 0, :]


def select_kernel(target_row, target_column, forcing, to_slots, to_columns, packed):
    slots, columns = to_slots.shape
    step = 256

    def body(index, _):
        rows = pl.ds(pl.multiple_of(index * step, step), step)
        place = lax.broadcasted_iota(jnp.int32, (step, columns), 0) + index * step
        picked = jnp.where(target_row[...] == place, 1.0, 0.0).astype(jnp.bfloat16)
        to_slots[rows, :] = picked
        packed[rows, :] = jnp.dot(
            picked, forcing[...], preferred_element_type=jnp.float32
        ).astype(jnp.bfloat16)
        place = lax.broadcasted_iota(jnp.int32, (step, slots), 1)
        to_columns[rows, :] = jnp.where(target_column[rows, :] == place, 1.0, 0.0).astype(
            jnp.bfloat16
        )
        return 0

    lax.fori_loop(0, slots // step, body, 0)


def advect_kernel(
    tracer,
    wind_x,
    wind_y,
    area_t,
    west,
    east,
    south,
    north,
    to_slots,
    packed_forcing,
    advected,
    features,
    rounded,
):
    cells_x, cells_y, levels = tracer.shape
    inverse = 1.0 / area_t[...]
    place = lax.broadcasted_iota(jnp.int32, (cells_y, levels), 0)
    west_speed = west[1]
    flux_before = jnp.maximum(west_speed, 0.0) * west[0] + jnp.minimum(west_speed, 0.0) * tracer[0]
    for i in range(cells_x):
        here = tracer[i]
        after = tracer[i + 1] if i + 1 < cells_x else east[...]
        speed = wind_x[i].astype(jnp.float32)
        flux_x = jnp.maximum(speed, 0.0) * here + jnp.minimum(speed, 0.0) * after
        speed = wind_y[i].astype(jnp.float32)
        beyond = jnp.where(
            place == cells_y - 1, north[i : i + 1, :], pltpu.roll(here, cells_y - 1, 0)
        )
        flux_y = jnp.maximum(speed, 0.0) * here + jnp.minimum(speed, 0.0) * beyond
        south_speed = south[1, i : i + 1, :]
        south_flux = (
            jnp.maximum(south_speed, 0.0) * south[0, i : i + 1, :]
            + jnp.minimum(south_speed, 0.0) * here[0:1, :]
        )
        flux_y_before = jnp.where(place == 0, south_flux, pltpu.roll(flux_y, 1, 0))
        spread = (flux_x - flux_before) + (flux_y - flux_y_before)
        moved = here - spread * inverse[:, i : i + 1]
        advected[i] = moved
        rounded[i * cells_y : (i + 1) * cells_y, :] = moved.astype(jnp.bfloat16)
        flux_before = flux_x
    features[:, levels:] = packed_forcing[...]
    features[:, :levels] = jnp.dot(
        to_slots[...], rounded[...], preferred_element_type=jnp.float32
    ).astype(jnp.bfloat16)


def net_kernel(rows_in, w_in, w_hidden, w_out, result):
    step = 256

    def leaky(values):
        return jnp.maximum(values, SLOPE * values).astype(jnp.bfloat16)

    def body(index, _):
        rows = pl.ds(pl.multiple_of(index * step, step), step)
        hidden = leaky(jnp.dot(rows_in[rows, :], w_in[0], preferred_element_type=jnp.float32))
        for layer in range(w_hidden.shape[1]):
            hidden = leaky(
                jnp.dot(hidden, w_hidden[0, layer], preferred_element_type=jnp.float32)
            )
        result[rows, :] = jnp.dot(
            hidden, w_out[0], preferred_element_type=jnp.float32
        ).astype(jnp.bfloat16)
        return 0

    lax.fori_loop(0, rows_in.shape[0] // step, body, 0)


def unpack_kernel(to_columns, returned, tendencies):
    step = 256

    def body(index, _):
        rows = pl.ds(pl.multiple_of(index * step, step), step)
        tendencies[rows, :] = jnp.dot(
            to_columns[rows, :], returned[...], preferred_element_type=jnp.float32
        ).astype(jnp.bfloat16)
        return 0

    lax.fori_loop(0, tendencies.shape[0] // step, body, 0)


def neighbours(axis):
    count = lax.axis_size(axis)
    forward = [(i, (i + 1) % count) for i in range(count)]
    return forward, [(target, source) for source, target in forward]


def local(tracer, wind_x, wind_y, cell_area, forcing, group_map, w_in, w_hidden, w_out):
    groups = lax.axis_size("blk")
    cells_x, cells_y, levels = tracer.shape
    columns = cells_x * cells_y
    slots_per = columns // groups
    width = levels + forcing.shape[2]
    width_out = w_out.shape[2]
    f32, bf16 = jnp.float32, jnp.bfloat16
    shaped = jax.ShapeDtypeStruct

    last_x, first_x, last_y, first_y = call(
        edges_kernel,
        [
            shaped((2, cells_y, levels), f32),
            shaped((cells_y, levels), f32),
            shaped((2, cells_x, levels), f32),
            shaped((cells_x, levels), f32),
        ],
        [tracer, wind_x, wind_y],
        "edges",
        touched=1 << 20,
    )
    forward, backward = neighbours("face")
    west = lax.ppermute(last_x, "face", forward)
    east = lax.ppermute(first_x, "face", backward)
    forward, backward = neighbours("blk")
    south = lax.ppermute(last_y, "blk", forward)
    north = lax.ppermute(first_y, "blk", backward)

    to_slots, to_columns, packed_forcing = call(
        select_kernel,
        [
            shaped((columns, columns), bf16),
            shaped((columns, columns), bf16),
            shaped((columns, forcing.shape[2]), bf16),
        ],
        [
            group_map.reshape(1, columns),
            group_map.reshape(columns, 1),
            forcing.reshape(columns, forcing.shape[2]),
        ],
        "select",
        flops=2 * columns * columns * forcing.shape[2],
        touched=6 << 20,
    )
    advected, features = call(
        advect_kernel,
        [shaped(tracer.shape, f32), shaped((columns, width), bf16)],
        [
            tracer,
            wind_x,
            wind_y,
            cell_area.T,
            west,
            east,
            south,
            north,
            to_slots,
            packed_forcing,
        ],
        "advect",
        flops=2 * columns * columns * levels,
        touched=6 << 20,
        scratch=[pltpu.VMEM((columns, levels), bf16)],
    )
    received = lax.all_to_all(
        features.reshape(groups, slots_per, width), "blk", split_axis=0, concat_axis=0, tiled=True
    )
    result = call(
        net_kernel,
        shaped((columns, width_out), bf16),
        [received.reshape(columns, width), w_in, w_hidden, w_out],
        "net",
        flops=2 * columns * (w_in.size + w_hidden.size + w_out.size),
        touched=5 << 20,
    )
    returned = lax.all_to_all(
        result.reshape(groups, slots_per, width_out), "blk", split_axis=0, concat_axis=0, tiled=True
    )
    tendencies = call(
        unpack_kernel,
        shaped((columns, width_out), bf16),
        [to_columns, returned.reshape(columns, width_out)],
        "unpack",
        flops=2 * columns * columns * width_out,
        touched=3 << 20,
    )
    return advected, tendencies.reshape(cells_x, cells_y, width_out)


def solution(mesh):
    placed = (
        P("face", "blk", None),
        P("face", "blk", None),
        P("face", "blk", None),
        P("face", "blk"),
        P("face", "blk", None),
        P("face", "blk"),
        P("blk", None, None),
        P("blk", None, None, None),
        P("blk", None, None),
    )
    return jax.shard_map(
        local,
        mesh=mesh,
        in_specs=placed,
        out_specs=(P("face", "blk", None), P("face", "blk", None)),
        check_vma=False,
    )
```

```python
import jax
import jax.numpy as jnp
from jax import lax
from jax.experimental import pallas as pl
from jax.experimental.pallas import tpu as pltpu
from jax.sharding import PartitionSpec as P

SLOPE = 0.15
VMEM = pl.BlockSpec(memory_space=pltpu.VMEM)


HBM = pl.BlockSpec(memory_space=pltpu.HBM)


def call(kernel, outs, operands, name, flops=0, touched=0, scratch=(), specs=None, limit=16 << 20):
    return pl.pallas_call(
        kernel,
        out_shape=outs,
        in_specs=specs or [VMEM] * len(operands),
        out_specs=jax.tree.map(lambda _: VMEM, outs),
        scratch_shapes=list(scratch),
        compiler_params=pltpu.CompilerParams(vmem_limit_bytes=limit),
        cost_estimate=pl.CostEstimate(flops=flops, bytes_accessed=touched, transcendentals=0),
        name=name,
    )(*operands)


def edges_kernel(
    tracer,
    wind_x,
    wind_y,
    last_x,
    first_x,
    last_y,
    first_y,
    low_rows,
    high_rows,
    speed_x,
    speed_y,
    arrived,
):
    cells_x, cells_y, _ = tracer.shape
    copies = [
        pltpu.make_async_copy(source, target, arrived.at[index])
        for index, (source, target) in enumerate(
            (
                (tracer.at[pl.ds(cells_x - 1, 1)], last_x.at[pl.ds(0, 1)]),
                (tracer.at[pl.ds(0, 1)], first_x),
                (wind_x.at[pl.ds(cells_x - 1, 1)], speed_x),
                (tracer.at[:, pl.ds(0, 8), :], low_rows),
                (tracer.at[:, pl.ds(cells_y - 8, 8), :], high_rows),
                (wind_y.at[:, pl.ds(cells_y - 16, 16), :], speed_y),
            )
        )
    ]
    for copy in copies:
        copy.start()
    for copy in copies:
        copy.wait()
    last_x[1] = speed_x[0].astype(jnp.float32)
    first_y[0] = low_rows[:, 0, :]
    last_y[0] = high_rows[:, 7, :]
    last_y[1] = speed_y[...].astype(jnp.float32)[:, 15, :]


def row_of(target, columns):
    cells_x, cells_y = target.shape
    lane = lax.broadcasted_iota(jnp.int32, (cells_y, columns), 1)
    place = lax.broadcasted_iota(jnp.int32, (cells_y, columns), 0)
    spread = jnp.where(lane % cells_y == place, 1.0, 0.0).astype(jnp.bfloat16)
    high = jnp.dot(
        (target >> 4).astype(jnp.float32).astype(jnp.bfloat16),
        spread,
        preferred_element_type=jnp.float32,
    )
    low = jnp.dot(
        (target & 15).astype(jnp.float32).astype(jnp.bfloat16),
        spread,
        preferred_element_type=jnp.float32,
    )
    lane = lax.broadcasted_iota(jnp.int32, (cells_x, columns), 1)
    place = lax.broadcasted_iota(jnp.int32, (cells_x, columns), 0)
    own = jnp.where(lane // cells_y == place, 16.0 * high + low, 0.0)
    return jnp.sum(own, axis=0, keepdims=True).astype(jnp.int32)


def select_kernel(target, forcing, to_slots, packed, rows, arrived):
    copy = pltpu.make_async_copy(forcing, rows, arrived)
    copy.start()
    slots, columns = to_slots.shape
    step = 128
    row = row_of(target[...], columns)

    def body(index, _):
        chunk = pl.ds(pl.multiple_of(index * step, step), step)
        place = lax.broadcasted_iota(jnp.int32, (step, columns), 0) + index * step
        to_slots[chunk, :] = jnp.where(row == place, 1.0, 0.0).astype(jnp.bfloat16)
        return 0

    lax.fori_loop(0, slots // step, body, 0)
    copy.wait()
    packed[...] = jnp.dot(
        to_slots[...], rows[...], preferred_element_type=jnp.float32
    ).astype(jnp.bfloat16)


def advect_kernel(
    tracer,
    wind_x,
    wind_y,
    area,
    west,
    east,
    south,
    north,
    to_slots,
    packed_forcing,
    advected,
    features,
    rounded,
):
    cells_x, cells_y, levels = tracer.shape
    inverse = jnp.transpose(1.0 / area[...])
    place = lax.broadcasted_iota(jnp.int32, (cells_y, levels), 0)
    west_speed = west[1]
    flux_before = jnp.maximum(west_speed, 0.0) * west[0] + jnp.minimum(west_speed, 0.0) * tracer[0]
    for i in range(cells_x):
        here = tracer[i]
        after = tracer[i + 1] if i + 1 < cells_x else east[0]
        speed = wind_x[i].astype(jnp.float32)
        flux_x = jnp.maximum(speed, 0.0) * here + jnp.minimum(speed, 0.0) * after
        speed = wind_y[i].astype(jnp.float32)
        beyond = jnp.where(
            place == cells_y - 1, north[0, i : i + 1, :], pltpu.roll(here, cells_y - 1, 0)
        )
        flux_y = jnp.maximum(speed, 0.0) * here + jnp.minimum(speed, 0.0) * beyond
        south_speed = south[1, i : i + 1, :]
        south_flux = (
            jnp.maximum(south_speed, 0.0) * south[0, i : i + 1, :]
            + jnp.minimum(south_speed, 0.0) * here[0:1, :]
        )
        flux_y_before = jnp.where(place == 0, south_flux, pltpu.roll(flux_y, 1, 0))
        spread = (flux_x - flux_before) + (flux_y - flux_y_before)
        moved = here - spread * inverse[:, i : i + 1]
        advected[i] = moved
        rounded[i * cells_y : (i + 1) * cells_y, :] = moved.astype(jnp.bfloat16)
        flux_before = flux_x
    features[:, levels:] = packed_forcing[...]
    features[:, :levels] = jnp.dot(
        to_slots[...], rounded[...], preferred_element_type=jnp.float32
    ).astype(jnp.bfloat16)


def net_kernel(rows_in, w_in, w_hidden, w_out, result, ping, pong):
    step = 256

    def leaky(values):
        return jnp.maximum(values, SLOPE * values)

    def layer(source, weights, target, finish):
        for start in range(0, source.shape[0], step):
            rows = slice(start, start + step)
            sums = jnp.dot(source[rows, :], weights, preferred_element_type=jnp.float32)
            target[rows, :] = finish(sums).astype(jnp.bfloat16)

    layer(rows_in, w_in[0], ping, leaky)
    here, there = ping, pong
    for index in range(w_hidden.shape[1]):
        layer(here, w_hidden[0, index], there, leaky)
        here, there = there, here
    layer(here, w_out[0], result, lambda sums: sums)


def unpack_kernel(target, returned, tendencies, to_columns):
    cells_x, cells_y = target.shape
    slots = returned.shape[0]
    turned = jnp.transpose(target[...].astype(jnp.float32)).astype(jnp.int32)
    place = lax.broadcasted_iota(jnp.int32, (cells_y, slots), 1)
    per = 8
    for first in range(0, cells_x, per):
        for i in range(first, first + per):
            to_columns[i * cells_y : (i + 1) * cells_y, :] = jnp.where(
                turned[:, i : i + 1] == place, 1.0, 0.0
            ).astype(jnp.bfloat16)
        rows = slice(first * cells_y, (first + per) * cells_y)
        tendencies[rows, :] = jnp.dot(
            to_columns[rows, :], returned[...], preferred_element_type=jnp.float32
        ).astype(jnp.bfloat16)


def neighbours(axis):
    count = lax.axis_size(axis)
    forward = [(i, (i + 1) % count) for i in range(count)]
    return forward, [(target, source) for source, target in forward]


def local(tracer, wind_x, wind_y, cell_area, forcing, group_map, w_in, w_hidden, w_out):
    groups = lax.axis_size("blk")
    cells_x, cells_y, levels = tracer.shape
    columns = cells_x * cells_y
    slots_per = columns // groups
    width = levels + forcing.shape[2]
    width_out = w_out.shape[2]
    f32, bf16 = jnp.float32, jnp.bfloat16
    shaped = jax.ShapeDtypeStruct

    last_x, first_x, last_y, first_y = call(
        edges_kernel,
        [
            shaped((2, cells_y, levels), f32),
            shaped((1, cells_y, levels), f32),
            shaped((2, cells_x, levels), f32),
            shaped((1, cells_x, levels), f32),
        ],
        [tracer, wind_x, wind_y],
        "edges",
        touched=1 << 19,
        scratch=[
            pltpu.VMEM((cells_x, 8, levels), f32),
            pltpu.VMEM((cells_x, 8, levels), f32),
            pltpu.VMEM((1, cells_y, levels), bf16),
            pltpu.VMEM((cells_x, 16, levels), bf16),
            pltpu.SemaphoreType.DMA((6,)),
        ],
        specs=[HBM] * 3,
        limit=60 << 20,
    )
    forward, backward = neighbours("face")
    west = lax.ppermute(last_x, "face", forward)
    east = lax.ppermute(first_x, "face", backward)
    forward, backward = neighbours("blk")
    south = lax.ppermute(last_y, "blk", forward)
    north = lax.ppermute(first_y, "blk", backward)

    to_slots, packed_forcing = call(
        select_kernel,
        [shaped((columns, columns), bf16), shaped((columns, forcing.shape[2]), bf16)],
        [group_map, forcing.reshape(columns, forcing.shape[2])],
        "select",
        flops=2 * columns * columns * forcing.shape[2],
        touched=4 << 20,
        scratch=[pltpu.VMEM((columns, forcing.shape[2]), bf16), pltpu.SemaphoreType.DMA],
        specs=[VMEM, HBM],
    )
    advected, features = call(
        advect_kernel,
        [shaped(tracer.shape, f32), shaped((columns, width), bf16)],
        [tracer, wind_x, wind_y, cell_area, west, east, south, north, to_slots, packed_forcing],
        "advect",
        flops=2 * columns * columns * levels,
        touched=6 << 20,
        scratch=[pltpu.VMEM((columns, levels), bf16)],
    )
    received = lax.all_to_all(
        features.reshape(groups, slots_per, width), "blk", split_axis=0, concat_axis=0, tiled=True
    )
    result = call(
        net_kernel,
        shaped((columns, width_out), bf16),
        [received.reshape(columns, width), w_in, w_hidden, w_out],
        "net",
        flops=2 * columns * (w_in.size + w_hidden.size + w_out.size),
        touched=5 << 20,
        scratch=[pltpu.VMEM((columns, w_in.shape[2]), bf16)] * 2,
    )
    returned = lax.all_to_all(
        result.reshape(groups, slots_per, width_out), "blk", split_axis=0, concat_axis=0, tiled=True
    )
    tendencies = call(
        unpack_kernel,
        shaped((columns, width_out), bf16),
        [group_map, returned.reshape(columns, width_out)],
        "unpack",
        flops=2 * columns * columns * width_out,
        touched=1 << 20,
        scratch=[pltpu.VMEM((columns, columns), bf16)],
    )
    return advected, tendencies.reshape(cells_x, cells_y, width_out)


def solution(mesh):
    placed = (
        P("face", "blk", None),
        P("face", "blk", None),
        P("face", "blk", None),
        P("face", "blk"),
        P("face", "blk", None),
        P("face", "blk"),
        P("blk", None, None),
        P("blk", None, None, None),
        P("blk", None, None),
    )
    return jax.shard_map(
        local,
        mesh=mesh,
        in_specs=placed,
        out_specs=(P("face", "blk", None), P("face", "blk", None)),
        check_vma=False,
    )
```

```python
import jax
import jax.numpy as jnp
from jax import lax
from jax.experimental import pallas as pl
from jax.experimental.pallas import tpu as pltpu
from jax.sharding import PartitionSpec as P

SLOPE = 0.15
VMEM = pl.BlockSpec(memory_space=pltpu.VMEM)


HBM = pl.BlockSpec(memory_space=pltpu.HBM)


def call(kernel, outs, operands, name, flops=0, touched=0, scratch=(), specs=None, out_specs=None):
    return pl.pallas_call(
        kernel,
        out_shape=outs,
        in_specs=specs or [VMEM] * len(operands),
        out_specs=out_specs or jax.tree.map(lambda _: VMEM, outs),
        scratch_shapes=list(scratch),
        compiler_params=pltpu.CompilerParams(vmem_limit_bytes=16 << 20),
        cost_estimate=pl.CostEstimate(flops=flops, bytes_accessed=touched, transcendentals=0),
        name=name,
    )(*operands)


def in_hbm(array):
    return pltpu.with_memory_space_constraint(array, pltpu.HBM)


def edges_kernel(
    tracer,
    wind_x,
    wind_y,
    target,
    last_x,
    first_x,
    last_y,
    first_y,
    held_target,
    low_rows,
    high_rows,
    speed_x,
    speed_y,
    arrived,
):
    cells_x, cells_y, _ = tracer.shape
    copies = [
        pltpu.make_async_copy(source, target, arrived.at[index])
        for index, (source, target) in enumerate(
            (
                (tracer.at[pl.ds(cells_x - 1, 1)], last_x.at[pl.ds(0, 1)]),
                (tracer.at[pl.ds(0, 1)], first_x.at[pl.ds(0, 1)]),
                (wind_x.at[pl.ds(cells_x - 1, 1)], speed_x),
                (tracer.at[:, pl.ds(0, 8), :], low_rows),
                (tracer.at[:, pl.ds(cells_y - 8, 8), :], high_rows),
                (wind_y.at[:, pl.ds(cells_y - 16, 16), :], speed_y),
                (target, held_target),
            )
        )
    ]
    for copy in copies:
        copy.start()
    first_x[1] = jnp.zeros(first_x.shape[1:], jnp.float32)
    first_y[1] = jnp.zeros(first_y.shape[1:], jnp.float32)
    for copy in copies:
        copy.wait()
    last_x[1] = speed_x[0].astype(jnp.float32)
    first_y[0] = low_rows[:, 0, :]
    last_y[0] = high_rows[:, 7, :]
    last_y[1] = speed_y[...].astype(jnp.float32)[:, 15, :]


def row_of(target, columns):
    cells_x, cells_y = target.shape
    lane = lax.broadcasted_iota(jnp.int32, (cells_y, columns), 1)
    place = lax.broadcasted_iota(jnp.int32, (cells_y, columns), 0)
    spread = jnp.where(lane % cells_y == place, 1.0, 0.0).astype(jnp.bfloat16)
    high = jnp.dot(
        (target >> 4).astype(jnp.float32).astype(jnp.bfloat16),
        spread,
        preferred_element_type=jnp.float32,
    )
    low = jnp.dot(
        (target & 15).astype(jnp.float32).astype(jnp.bfloat16),
        spread,
        preferred_element_type=jnp.float32,
    )
    lane = lax.broadcasted_iota(jnp.int32, (cells_x, columns), 1)
    place = lax.broadcasted_iota(jnp.int32, (cells_x, columns), 0)
    own = jnp.where(lane // cells_y == place, 16.0 * high + low, 0.0)
    return jnp.sum(own, axis=0, keepdims=True).astype(jnp.int32)


def select_kernel(target, forcing, to_slots, packed, rows, arrived):
    copy = pltpu.make_async_copy(forcing, rows, arrived)
    copy.start()
    slots, columns = to_slots.shape
    step = 128
    row = row_of(target[...], columns)

    def body(index, _):
        chunk = pl.ds(pl.multiple_of(index * step, step), step)
        place = lax.broadcasted_iota(jnp.int32, (step, columns), 0) + index * step
        to_slots[chunk, :] = jnp.where(row == place, 1.0, 0.0).astype(jnp.bfloat16)
        return 0

    lax.fori_loop(0, slots // step, body, 0)
    copy.wait()
    packed[...] = jnp.dot(
        to_slots[...], rows[...], preferred_element_type=jnp.float32
    ).astype(jnp.bfloat16)


def advect_kernel(
    tracer,
    wind_x,
    wind_y,
    area,
    south,
    north,
    west,
    east,
    to_slots,
    packed_forcing,
    advected,
    features,
    rounded,
):
    cells_x, cells_y, levels = tracer.shape
    inverse = jnp.transpose(1.0 / area[...])
    place = lax.broadcasted_iota(jnp.int32, (cells_y, levels), 0)
    west_speed = west[1]
    flux_before = jnp.maximum(west_speed, 0.0) * west[0] + jnp.minimum(west_speed, 0.0) * tracer[0]
    for i in range(cells_x):
        here = tracer[i]
        after = tracer[i + 1] if i + 1 < cells_x else east[0]
        speed = wind_x[i].astype(jnp.float32)
        flux_x = jnp.maximum(speed, 0.0) * here + jnp.minimum(speed, 0.0) * after
        speed = wind_y[i].astype(jnp.float32)
        beyond = jnp.where(
            place == cells_y - 1, north[0, i : i + 1, :], pltpu.roll(here, cells_y - 1, 0)
        )
        flux_y = jnp.maximum(speed, 0.0) * here + jnp.minimum(speed, 0.0) * beyond
        south_speed = south[1, i : i + 1, :]
        south_flux = (
            jnp.maximum(south_speed, 0.0) * south[0, i : i + 1, :]
            + jnp.minimum(south_speed, 0.0) * here[0:1, :]
        )
        flux_y_before = jnp.where(place == 0, south_flux, pltpu.roll(flux_y, 1, 0))
        spread = (flux_x - flux_before) + (flux_y - flux_y_before)
        moved = here - spread * inverse[:, i : i + 1]
        advected[i] = moved
        rounded[i * cells_y : (i + 1) * cells_y, :] = moved.astype(jnp.bfloat16)
        flux_before = flux_x
    features[:, levels:] = packed_forcing[...]
    features[:, :levels] = jnp.dot(
        to_slots[...], rounded[...], preferred_element_type=jnp.float32
    ).astype(jnp.bfloat16)


def net_kernel(
    rows_in, w_in, w_hidden, w_out, advected, result, advected_out, ping, pong, stored
):
    step = 256
    copy = pltpu.make_async_copy(advected, advected_out, stored)
    copy.start()

    def leaky(values):
        return jnp.maximum(values, SLOPE * values)

    def layer(source, weights, target, finish):
        for start in range(0, source.shape[0], step):
            rows = slice(start, start + step)
            sums = jnp.dot(source[rows, :], weights, preferred_element_type=jnp.float32)
            target[rows, :] = finish(sums).astype(jnp.bfloat16)

    layer(rows_in, w_in[0], ping, leaky)
    here, there = ping, pong
    for index in range(w_hidden.shape[1]):
        layer(here, w_hidden[0, index], there, leaky)
        here, there = there, here
    layer(here, w_out[0], result, lambda sums: sums)
    copy.wait()


def unpack_kernel(target, returned, tendencies, to_columns):
    cells_x, cells_y = target.shape
    slots = returned.shape[0]
    turned = jnp.transpose(target[...].astype(jnp.float32)).astype(jnp.int32)
    place = lax.broadcasted_iota(jnp.int32, (cells_y, slots), 1)
    per = 8
    for first in range(0, cells_x, per):
        for i in range(first, first + per):
            to_columns[i * cells_y : (i + 1) * cells_y, :] = jnp.where(
                turned[:, i : i + 1] == place, 1.0, 0.0
            ).astype(jnp.bfloat16)
        rows = slice(first * cells_y, (first + per) * cells_y)
        tendencies[rows, :] = jnp.dot(
            to_columns[rows, :], returned[...], preferred_element_type=jnp.float32
        ).astype(jnp.bfloat16)


def neighbours(axis):
    count = lax.axis_size(axis)
    forward = [(i, (i + 1) % count) for i in range(count)]
    return forward, [(target, source) for source, target in forward]


def local(tracer, wind_x, wind_y, cell_area, forcing, group_map, w_in, w_hidden, w_out):
    groups = lax.axis_size("blk")
    cells_x, cells_y, levels = tracer.shape
    columns = cells_x * cells_y
    slots_per = columns // groups
    width = levels + forcing.shape[2]
    width_out = w_out.shape[2]
    f32, bf16 = jnp.float32, jnp.bfloat16
    shaped = pltpu.VMEM
    result_of = jax.ShapeDtypeStruct

    last_x, first_x, last_y, first_y, target = call(
        edges_kernel,
        [
            shaped((2, cells_y, levels), f32),
            shaped((2, cells_y, levels), f32),
            shaped((2, cells_x, levels), f32),
            shaped((2, cells_x, levels), f32),
            shaped(group_map.shape, group_map.dtype),
        ],
        [in_hbm(tracer), in_hbm(wind_x), in_hbm(wind_y), in_hbm(group_map)],
        "edges",
        touched=1 << 19,
        scratch=[
            pltpu.VMEM((cells_x, 8, levels), f32),
            pltpu.VMEM((cells_x, 8, levels), f32),
            pltpu.VMEM((1, cells_y, levels), bf16),
            pltpu.VMEM((cells_x, 16, levels), bf16),
            pltpu.SemaphoreType.DMA((7,)),
        ],
        specs=[HBM] * 4,
    )
    forward, backward = neighbours("face")
    west = lax.ppermute(last_x, "face", forward)
    east = lax.ppermute(first_x, "face", backward)
    forward, backward = neighbours("blk")
    south = lax.ppermute(last_y, "blk", forward)
    north = lax.ppermute(first_y, "blk", backward)

    to_slots, packed_forcing = call(
        select_kernel,
        [shaped((columns, columns), bf16), shaped((columns, forcing.shape[2]), bf16)],
        [target, in_hbm(forcing.reshape(columns, forcing.shape[2]))],
        "select",
        flops=2 * columns * columns * forcing.shape[2],
        touched=4 << 20,
        scratch=[pltpu.VMEM((columns, forcing.shape[2]), bf16), pltpu.SemaphoreType.DMA],
        specs=[VMEM, HBM],
    )
    advected, features = call(
        advect_kernel,
        [shaped(tracer.shape, f32), shaped((columns, width), bf16)],
        [tracer, wind_x, wind_y, cell_area, south, north, west, east, to_slots, packed_forcing],
        "advect",
        flops=2 * columns * columns * levels,
        touched=6 << 20,
        scratch=[pltpu.VMEM((columns, levels), bf16)],
    )
    received = lax.all_to_all(
        features.reshape(groups, slots_per, width), "blk", split_axis=0, concat_axis=0, tiled=True
    )
    result, advected = call(
        net_kernel,
        [shaped((columns, width_out), bf16), result_of(tracer.shape, f32)],
        [received.reshape(columns, width), w_in, w_hidden, w_out, advected],
        "net",
        flops=2 * columns * (w_in.size + w_hidden.size + w_out.size),
        touched=5 << 20,
        scratch=[pltpu.VMEM((columns, w_in.shape[2]), bf16)] * 2 + [pltpu.SemaphoreType.DMA],
        out_specs=[VMEM, HBM],
    )
    returned = lax.all_to_all(
        result.reshape(groups, slots_per, width_out), "blk", split_axis=0, concat_axis=0, tiled=True
    )
    tendencies = call(
        unpack_kernel,
        result_of((columns, width_out), bf16),
        [target, returned.reshape(columns, width_out)],
        "unpack",
        flops=2 * columns * columns * width_out,
        touched=1 << 20,
        scratch=[pltpu.VMEM((columns, columns), bf16)],
    )
    return advected, tendencies.reshape(cells_x, cells_y, width_out)


def solution(mesh):
    placed = (
        P("face", "blk", None),
        P("face", "blk", None),
        P("face", "blk", None),
        P("face", "blk"),
        P("face", "blk", None),
        P("face", "blk"),
        P("blk", None, None),
        P("blk", None, None, None),
        P("blk", None, None),
    )
    return jax.shard_map(
        local,
        mesh=mesh,
        in_specs=placed,
        out_specs=(P("face", "blk", None), P("face", "blk", None)),
        check_vma=False,
    )
```

```python
import jax
import jax.numpy as jnp
from jax import lax
from jax.experimental import pallas as pl
from jax.experimental.pallas import tpu as pltpu
from jax.sharding import PartitionSpec as P

SLOPE = 0.15
VMEM = pl.BlockSpec(memory_space=pltpu.VMEM)


HBM = pl.BlockSpec(memory_space=pltpu.HBM)


def call(kernel, outs, operands, name, flops=0, touched=0, scratch=(), specs=None, out_specs=None):
    return pl.pallas_call(
        kernel,
        out_shape=outs,
        in_specs=specs or [VMEM] * len(operands),
        out_specs=out_specs or jax.tree.map(lambda _: VMEM, outs),
        scratch_shapes=list(scratch),
        compiler_params=pltpu.CompilerParams(vmem_limit_bytes=16 << 20),
        cost_estimate=pl.CostEstimate(flops=flops, bytes_accessed=touched, transcendentals=0),
        name=name,
    )(*operands)


def in_hbm(array):
    return pltpu.with_memory_space_constraint(array, pltpu.HBM)


def edges_kernel(
    tracer,
    wind_x,
    wind_y,
    target,
    last_x,
    first_x,
    last_y,
    first_y,
    held_target,
    low_rows,
    high_rows,
    speed_x,
    speed_y,
    arrived,
):
    cells_x, cells_y, _ = tracer.shape
    copies = [
        pltpu.make_async_copy(source, target, arrived.at[index])
        for index, (source, target) in enumerate(
            (
                (tracer.at[pl.ds(cells_x - 1, 1)], last_x.at[pl.ds(0, 1)]),
                (tracer.at[pl.ds(0, 1)], first_x.at[pl.ds(0, 1)]),
                (wind_x.at[pl.ds(cells_x - 1, 1)], speed_x),
                (tracer.at[:, pl.ds(0, 8), :], low_rows),
                (tracer.at[:, pl.ds(cells_y - 8, 8), :], high_rows),
                (wind_y.at[:, pl.ds(cells_y - 16, 16), :], speed_y),
                (target, held_target),
            )
        )
    ]
    for copy in copies:
        copy.start()
    first_x[1] = jnp.zeros(first_x.shape[1:], jnp.float32)
    first_y[1] = jnp.zeros(first_y.shape[1:], jnp.float32)
    for copy in copies:
        copy.wait()
    last_x[1] = speed_x[0].astype(jnp.float32)
    first_y[0] = low_rows[:, 0, :]
    last_y[0] = high_rows[:, 7, :]
    last_y[1] = speed_y[...].astype(jnp.float32)[:, 15, :]


def row_of(target, columns):
    cells_x, cells_y = target.shape
    lane = lax.broadcasted_iota(jnp.int32, (cells_y, columns), 1)
    place = lax.broadcasted_iota(jnp.int32, (cells_y, columns), 0)
    spread = jnp.where(lane % cells_y == place, 1.0, 0.0).astype(jnp.bfloat16)
    high = jnp.dot(
        (target >> 4).astype(jnp.float32).astype(jnp.bfloat16),
        spread,
        preferred_element_type=jnp.float32,
    )
    low = jnp.dot(
        (target & 15).astype(jnp.float32).astype(jnp.bfloat16),
        spread,
        preferred_element_type=jnp.float32,
    )
    lane = lax.broadcasted_iota(jnp.int32, (cells_x, columns), 1)
    place = lax.broadcasted_iota(jnp.int32, (cells_x, columns), 0)
    own = jnp.where(lane // cells_y == place, 16.0 * high + low, 0.0)
    return jnp.sum(own, axis=0, keepdims=True).astype(jnp.int32)


def select_kernel(target, forcing, to_slots, packed, rows, arrived):
    copy = pltpu.make_async_copy(forcing, rows, arrived)
    copy.start()
    slots, columns = to_slots.shape
    step = 128
    row = row_of(target[...], columns)

    def body(index, _):
        chunk = pl.ds(pl.multiple_of(index * step, step), step)
        place = lax.broadcasted_iota(jnp.int32, (step, columns), 0) + index * step
        to_slots[chunk, :] = jnp.where(row == place, 1.0, 0.0).astype(jnp.bfloat16)
        return 0

    lax.fori_loop(0, slots // step, body, 0)
    copy.wait()
    packed[...] = jnp.dot(
        to_slots[...], rows[...], preferred_element_type=jnp.float32
    ).astype(jnp.bfloat16)


def advect_kernel(
    tracer,
    wind_x,
    wind_y,
    area,
    west,
    east,
    south,
    north,
    to_slots,
    packed_forcing,
    advected,
    features,
    rounded,
):
    cells_x, cells_y, levels = tracer.shape
    inverse = jnp.transpose(1.0 / area[...])
    place = lax.broadcasted_iota(jnp.int32, (cells_y, levels), 0)
    west_speed = west[1]
    flux_before = jnp.maximum(west_speed, 0.0) * west[0] + jnp.minimum(west_speed, 0.0) * tracer[0]
    for i in range(cells_x):
        here = tracer[i]
        after = tracer[i + 1] if i + 1 < cells_x else east[0]
        speed = wind_x[i].astype(jnp.float32)
        flux_x = jnp.maximum(speed, 0.0) * here + jnp.minimum(speed, 0.0) * after
        speed = wind_y[i].astype(jnp.float32)
        beyond = jnp.where(
            place == cells_y - 1, north[0, i : i + 1, :], pltpu.roll(here, cells_y - 1, 0)
        )
        flux_y = jnp.maximum(speed, 0.0) * here + jnp.minimum(speed, 0.0) * beyond
        south_speed = south[1, i : i + 1, :]
        south_flux = (
            jnp.maximum(south_speed, 0.0) * south[0, i : i + 1, :]
            + jnp.minimum(south_speed, 0.0) * here[0:1, :]
        )
        flux_y_before = jnp.where(place == 0, south_flux, pltpu.roll(flux_y, 1, 0))
        spread = (flux_x - flux_before) + (flux_y - flux_y_before)
        moved = here - spread * inverse[:, i : i + 1]
        advected[i] = moved
        rounded[i * cells_y : (i + 1) * cells_y, :] = moved.astype(jnp.bfloat16)
        flux_before = flux_x
    features[:, levels:] = packed_forcing[...]
    features[:, :levels] = jnp.dot(
        to_slots[...], rounded[...], preferred_element_type=jnp.float32
    ).astype(jnp.bfloat16)


def net_kernel(
    rows_in, w_in, w_hidden, w_out, advected, result, advected_out, ping, pong, stored
):
    step = 256
    copy = pltpu.make_async_copy(advected, advected_out, stored)
    copy.start()

    def leaky(values):
        return jnp.maximum(values, SLOPE * values)

    def layer(source, weights, target, finish):
        for start in range(0, source.shape[0], step):
            rows = slice(start, start + step)
            sums = jnp.dot(source[rows, :], weights, preferred_element_type=jnp.float32)
            target[rows, :] = finish(sums).astype(jnp.bfloat16)

    layer(rows_in, w_in[0], ping, leaky)
    here, there = ping, pong
    for index in range(w_hidden.shape[1]):
        layer(here, w_hidden[0, index], there, leaky)
        here, there = there, here
    layer(here, w_out[0], result, lambda sums: sums)
    copy.wait()


def unpack_kernel(target, returned, tendencies, to_columns):
    cells_x, cells_y = target.shape
    slots = returned.shape[0]
    turned = jnp.transpose(target[...].astype(jnp.float32)).astype(jnp.int32)
    place = lax.broadcasted_iota(jnp.int32, (cells_y, slots), 1)
    per = 8
    for first in range(0, cells_x, per):
        for i in range(first, first + per):
            to_columns[i * cells_y : (i + 1) * cells_y, :] = jnp.where(
                turned[:, i : i + 1] == place, 1.0, 0.0
            ).astype(jnp.bfloat16)
        rows = slice(first * cells_y, (first + per) * cells_y)
        tendencies[rows, :] = jnp.dot(
            to_columns[rows, :], returned[...], preferred_element_type=jnp.float32
        ).astype(jnp.bfloat16)


def neighbours(axis):
    count = lax.axis_size(axis)
    forward = [(i, (i + 1) % count) for i in range(count)]
    return forward, [(target, source) for source, target in forward]


def local(tracer, wind_x, wind_y, cell_area, forcing, group_map, w_in, w_hidden, w_out):
    groups = lax.axis_size("blk")
    cells_x, cells_y, levels = tracer.shape
    columns = cells_x * cells_y
    slots_per = columns // groups
    width = levels + forcing.shape[2]
    width_out = w_out.shape[2]
    f32, bf16 = jnp.float32, jnp.bfloat16
    shaped = pltpu.VMEM
    result_of = jax.ShapeDtypeStruct

    last_x, first_x, last_y, first_y, target = call(
        edges_kernel,
        [
            shaped((2, cells_y, levels), f32),
            shaped((2, cells_y, levels), f32),
            shaped((2, cells_x, levels), f32),
            shaped((2, cells_x, levels), f32),
            shaped(group_map.shape, group_map.dtype),
        ],
        [in_hbm(tracer), in_hbm(wind_x), in_hbm(wind_y), in_hbm(group_map)],
        "edges",
        touched=1 << 19,
        scratch=[
            pltpu.VMEM((cells_x, 8, levels), f32),
            pltpu.VMEM((cells_x, 8, levels), f32),
            pltpu.VMEM((1, cells_y, levels), bf16),
            pltpu.VMEM((cells_x, 16, levels), bf16),
            pltpu.SemaphoreType.DMA((7,)),
        ],
        specs=[HBM] * 4,
    )
    forward, backward = neighbours("face")
    west = lax.ppermute(last_x, "face", forward)
    east = lax.ppermute(first_x, "face", backward)
    forward, backward = neighbours("blk")
    south = lax.ppermute(last_y, "blk", forward)
    north = lax.ppermute(first_y, "blk", backward)

    to_slots, packed_forcing = call(
        select_kernel,
        [shaped((columns, columns), bf16), shaped((columns, forcing.shape[2]), bf16)],
        [target, in_hbm(forcing.reshape(columns, forcing.shape[2]))],
        "select",
        flops=2 * columns * columns * forcing.shape[2],
        touched=4 << 20,
        scratch=[pltpu.VMEM((columns, forcing.shape[2]), bf16), pltpu.SemaphoreType.DMA],
        specs=[VMEM, HBM],
    )
    advected, features = call(
        advect_kernel,
        [shaped(tracer.shape, f32), shaped((columns, width), bf16)],
        [tracer, wind_x, wind_y, cell_area, west, east, south, north, to_slots, packed_forcing],
        "advect",
        flops=2 * columns * columns * levels,
        touched=6 << 20,
        scratch=[pltpu.VMEM((columns, levels), bf16)],
    )
    received = lax.all_to_all(
        features.reshape(groups, slots_per, width), "blk", split_axis=0, concat_axis=0, tiled=True
    )
    result, advected = call(
        net_kernel,
        [shaped((columns, width_out), bf16), result_of(tracer.shape, f32)],
        [received.reshape(columns, width), w_in, w_hidden, w_out, advected],
        "net",
        flops=2 * columns * (w_in.size + w_hidden.size + w_out.size),
        touched=5 << 20,
        scratch=[pltpu.VMEM((columns, w_in.shape[2]), bf16)] * 2 + [pltpu.SemaphoreType.DMA],
        out_specs=[VMEM, HBM],
    )
    returned = lax.all_to_all(
        result.reshape(groups, slots_per, width_out), "blk", split_axis=0, concat_axis=0, tiled=True
    )
    tendencies = call(
        unpack_kernel,
        result_of((columns, width_out), bf16),
        [target, returned.reshape(columns, width_out)],
        "unpack",
        flops=2 * columns * columns * width_out,
        touched=1 << 20,
        scratch=[pltpu.VMEM((columns, columns), bf16)],
    )
    return advected, tendencies.reshape(cells_x, cells_y, width_out)


def solution(mesh):
    placed = (
        P("face", "blk", None),
        P("face", "blk", None),
        P("face", "blk", None),
        P("face", "blk"),
        P("face", "blk", None),
        P("face", "blk"),
        P("blk", None, None),
        P("blk", None, None, None),
        P("blk", None, None),
    )
    return jax.shard_map(
        local,
        mesh=mesh,
        in_specs=placed,
        out_specs=(P("face", "blk", None), P("face", "blk", None)),
        check_vma=False,
    )
```

```python
import jax
import jax.numpy as jnp
from jax import lax
from jax.experimental import pallas as pl
from jax.experimental.pallas import tpu as pltpu
from jax.sharding import PartitionSpec as P

SLOPE = 0.15
VMEM = pl.BlockSpec(memory_space=pltpu.VMEM)


HBM = pl.BlockSpec(memory_space=pltpu.HBM)


def call(kernel, outs, operands, name, flops=0, touched=0, scratch=(), specs=None, out_specs=None):
    return pl.pallas_call(
        kernel,
        out_shape=outs,
        in_specs=specs or [VMEM] * len(operands),
        out_specs=out_specs or jax.tree.map(lambda _: VMEM, outs),
        scratch_shapes=list(scratch),
        compiler_params=pltpu.CompilerParams(vmem_limit_bytes=16 << 20),
        cost_estimate=pl.CostEstimate(flops=flops, bytes_accessed=touched, transcendentals=0),
        name=name,
    )(*operands)


def in_hbm(array):
    return pltpu.with_memory_space_constraint(array, pltpu.HBM)


def edges_kernel(
    tracer,
    wind_x,
    wind_y,
    target,
    last_x,
    first_x,
    last_y,
    first_y,
    held_target,
    low_rows,
    high_rows,
    speed_x,
    speed_y,
    arrived,
):
    cells_x, cells_y, _ = tracer.shape
    copies = [
        pltpu.make_async_copy(source, target, arrived.at[index])
        for index, (source, target) in enumerate(
            (
                (tracer.at[pl.ds(cells_x - 1, 1)], last_x.at[pl.ds(0, 1)]),
                (tracer.at[pl.ds(0, 1)], first_x.at[pl.ds(0, 1)]),
                (wind_x.at[pl.ds(cells_x - 1, 1)], speed_x),
                (tracer.at[:, pl.ds(0, 8), :], low_rows),
                (tracer.at[:, pl.ds(cells_y - 8, 8), :], high_rows),
                (wind_y.at[:, pl.ds(cells_y - 16, 16), :], speed_y),
                (target, held_target),
            )
        )
    ]
    for copy in copies:
        copy.start()
    first_x[1] = jnp.zeros(first_x.shape[1:], jnp.float32)
    first_y[1] = jnp.zeros(first_y.shape[1:], jnp.float32)
    for copy in copies:
        copy.wait()
    last_x[1] = speed_x[0].astype(jnp.float32)
    first_y[0] = low_rows[:, 0, :]
    last_y[0] = high_rows[:, 7, :]
    last_y[1] = speed_y[...].astype(jnp.float32)[:, 15, :]


def row_of(target, columns):
    cells_x, cells_y = target.shape
    lane = lax.broadcasted_iota(jnp.int32, (cells_y, columns), 1)
    place = lax.broadcasted_iota(jnp.int32, (cells_y, columns), 0)
    spread = jnp.where(lane % cells_y == place, 1.0, 0.0).astype(jnp.bfloat16)
    high = jnp.dot(
        (target >> 4).astype(jnp.float32).astype(jnp.bfloat16),
        spread,
        preferred_element_type=jnp.float32,
    )
    low = jnp.dot(
        (target & 15).astype(jnp.float32).astype(jnp.bfloat16),
        spread,
        preferred_element_type=jnp.float32,
    )
    lane = lax.broadcasted_iota(jnp.int32, (cells_x, columns), 1)
    place = lax.broadcasted_iota(jnp.int32, (cells_x, columns), 0)
    own = jnp.where(lane // cells_y == place, 16.0 * high + low, 0.0)
    return jnp.sum(own, axis=0, keepdims=True).astype(jnp.int32)


def fill_slots(target, to_slots):
    slots, columns = to_slots.shape
    step = 128
    row = row_of(target[...], columns)

    def body(index, _):
        chunk = pl.ds(pl.multiple_of(index * step, step), step)
        place = lax.broadcasted_iota(jnp.int32, (step, columns), 0) + index * step
        to_slots[chunk, :] = jnp.where(row == place, 1.0, 0.0).astype(jnp.bfloat16)
        return 0

    lax.fori_loop(0, slots // step, body, 0)


def select_kernel(target, forcing, to_slots, packed, rows, arrived):
    @pl.when(lax.axis_index("face") % 2 == 1)
    def _():
        copy = pltpu.make_async_copy(forcing, rows, arrived)
        copy.start()
        fill_slots(target, to_slots)
        copy.wait()
        packed[...] = jnp.dot(
            to_slots[...], rows[...], preferred_element_type=jnp.float32
        ).astype(jnp.bfloat16)


def advect_kernel(
    tracer,
    wind_x,
    wind_y,
    area,
    west,
    east,
    south,
    north,
    to_slots,
    packed_forcing,
    target,
    forcing,
    advected,
    features,
    rounded,
    own_slots,
    rows,
    arrived,
):
    cells_x, cells_y, levels = tracer.shape
    second = lax.axis_index("face") % 2 == 0
    copy = pltpu.make_async_copy(forcing, rows, arrived)

    @pl.when(second)
    def _():
        copy.start()

    inverse = jnp.transpose(1.0 / area[...])
    place = lax.broadcasted_iota(jnp.int32, (cells_y, levels), 0)
    west_speed = west[1]
    flux_before = jnp.maximum(west_speed, 0.0) * west[0] + jnp.minimum(west_speed, 0.0) * tracer[0]
    for i in range(cells_x):
        here = tracer[i]
        after = tracer[i + 1] if i + 1 < cells_x else east[0]
        speed = wind_x[i].astype(jnp.float32)
        flux_x = jnp.maximum(speed, 0.0) * here + jnp.minimum(speed, 0.0) * after
        speed = wind_y[i].astype(jnp.float32)
        beyond = jnp.where(
            place == cells_y - 1, north[0, i : i + 1, :], pltpu.roll(here, cells_y - 1, 0)
        )
        flux_y = jnp.maximum(speed, 0.0) * here + jnp.minimum(speed, 0.0) * beyond
        south_speed = south[1, i : i + 1, :]
        south_flux = (
            jnp.maximum(south_speed, 0.0) * south[0, i : i + 1, :]
            + jnp.minimum(south_speed, 0.0) * here[0:1, :]
        )
        flux_y_before = jnp.where(place == 0, south_flux, pltpu.roll(flux_y, 1, 0))
        spread = (flux_x - flux_before) + (flux_y - flux_y_before)
        moved = here - spread * inverse[:, i : i + 1]
        advected[i] = moved
        rounded[i * cells_y : (i + 1) * cells_y, :] = moved.astype(jnp.bfloat16)
        flux_before = flux_x

    def put(part, values):
        features[:, part] = values.astype(jnp.bfloat16)

    @pl.when(jnp.logical_not(second))
    def _():
        features[:, levels:] = packed_forcing[...]
        put(
            slice(0, levels),
            jnp.dot(to_slots[...], rounded[...], preferred_element_type=jnp.float32),
        )

    @pl.when(second)
    def _():
        fill_slots(target, own_slots)
        put(
            slice(0, levels),
            jnp.dot(own_slots[...], rounded[...], preferred_element_type=jnp.float32),
        )
        copy.wait()
        put(
            slice(levels, features.shape[1]),
            jnp.dot(own_slots[...], rows[...], preferred_element_type=jnp.float32),
        )


def net_kernel(
    rows_in, w_in, w_hidden, w_out, advected, result, advected_out, ping, pong, stored
):
    step = 256
    copy = pltpu.make_async_copy(advected, advected_out, stored)
    copy.start()

    def leaky(values):
        return jnp.maximum(values, SLOPE * values)

    def layer(source, weights, target, finish):
        for start in range(0, source.shape[0], step):
            rows = slice(start, start + step)
            sums = jnp.dot(source[rows, :], weights, preferred_element_type=jnp.float32)
            target[rows, :] = finish(sums).astype(jnp.bfloat16)

    layer(rows_in, w_in[0], ping, leaky)
    here, there = ping, pong
    for index in range(w_hidden.shape[1]):
        layer(here, w_hidden[0, index], there, leaky)
        here, there = there, here
    layer(here, w_out[0], result, lambda sums: sums)
    copy.wait()


def unpack_kernel(target, returned, tendencies, to_columns):
    cells_x, cells_y = target.shape
    slots = returned.shape[0]
    turned = jnp.transpose(target[...].astype(jnp.float32)).astype(jnp.int32)
    place = lax.broadcasted_iota(jnp.int32, (cells_y, slots), 1)
    per = 8
    for first in range(0, cells_x, per):
        for i in range(first, first + per):
            to_columns[i * cells_y : (i + 1) * cells_y, :] = jnp.where(
                turned[:, i : i + 1] == place, 1.0, 0.0
            ).astype(jnp.bfloat16)
        rows = slice(first * cells_y, (first + per) * cells_y)
        tendencies[rows, :] = jnp.dot(
            to_columns[rows, :], returned[...], preferred_element_type=jnp.float32
        ).astype(jnp.bfloat16)


def neighbours(axis):
    count = lax.axis_size(axis)
    forward = [(i, (i + 1) % count) for i in range(count)]
    return forward, [(target, source) for source, target in forward]


def local(tracer, wind_x, wind_y, cell_area, forcing, group_map, w_in, w_hidden, w_out):
    groups = lax.axis_size("blk")
    cells_x, cells_y, levels = tracer.shape
    columns = cells_x * cells_y
    slots_per = columns // groups
    width = levels + forcing.shape[2]
    width_out = w_out.shape[2]
    f32, bf16 = jnp.float32, jnp.bfloat16
    shaped = pltpu.VMEM
    result_of = jax.ShapeDtypeStruct

    last_x, first_x, last_y, first_y, target = call(
        edges_kernel,
        [
            shaped((2, cells_y, levels), f32),
            shaped((2, cells_y, levels), f32),
            shaped((2, cells_x, levels), f32),
            shaped((2, cells_x, levels), f32),
            shaped(group_map.shape, group_map.dtype),
        ],
        [in_hbm(tracer), in_hbm(wind_x), in_hbm(wind_y), in_hbm(group_map)],
        "edges",
        touched=1 << 19,
        scratch=[
            pltpu.VMEM((cells_x, 8, levels), f32),
            pltpu.VMEM((cells_x, 8, levels), f32),
            pltpu.VMEM((1, cells_y, levels), bf16),
            pltpu.VMEM((cells_x, 16, levels), bf16),
            pltpu.SemaphoreType.DMA((7,)),
        ],
        specs=[HBM] * 4,
    )
    forward, backward = neighbours("face")
    west = lax.ppermute(last_x, "face", forward)
    east = lax.ppermute(first_x, "face", backward)
    forward, backward = neighbours("blk")
    south = lax.ppermute(last_y, "blk", forward)
    north = lax.ppermute(first_y, "blk", backward)

    to_slots, packed_forcing = call(
        select_kernel,
        [shaped((columns, columns), bf16), shaped((columns, forcing.shape[2]), bf16)],
        [target, in_hbm(forcing.reshape(columns, forcing.shape[2]))],
        "select",
        flops=2 * columns * columns * forcing.shape[2],
        touched=4 << 20,
        scratch=[pltpu.VMEM((columns, forcing.shape[2]), bf16), pltpu.SemaphoreType.DMA],
        specs=[VMEM, HBM],
    )
    advected, features = call(
        advect_kernel,
        [shaped(tracer.shape, f32), shaped((columns, width), bf16)],
        [
            tracer,
            wind_x,
            wind_y,
            cell_area,
            west,
            east,
            south,
            north,
            to_slots,
            packed_forcing,
            target,
            in_hbm(forcing.reshape(columns, forcing.shape[2])),
        ],
        "advect",
        flops=2 * columns * columns * levels,
        touched=6 << 20,
        scratch=[
            pltpu.VMEM((columns, levels), bf16),
            pltpu.VMEM((columns, columns), bf16),
            pltpu.VMEM((columns, forcing.shape[2]), bf16),
            pltpu.SemaphoreType.DMA,
        ],
        specs=[VMEM] * 11 + [HBM],
    )
    received = lax.all_to_all(
        features.reshape(groups, slots_per, width), "blk", split_axis=0, concat_axis=0, tiled=True
    )
    result, advected = call(
        net_kernel,
        [shaped((columns, width_out), bf16), result_of(tracer.shape, f32)],
        [received.reshape(columns, width), w_in, w_hidden, w_out, advected],
        "net",
        flops=2 * columns * (w_in.size + w_hidden.size + w_out.size),
        touched=5 << 20,
        scratch=[pltpu.VMEM((columns, w_in.shape[2]), bf16)] * 2 + [pltpu.SemaphoreType.DMA],
        out_specs=[VMEM, HBM],
    )
    returned = lax.all_to_all(
        result.reshape(groups, slots_per, width_out), "blk", split_axis=0, concat_axis=0, tiled=True
    )
    tendencies = call(
        unpack_kernel,
        result_of((columns, width_out), bf16),
        [target, returned.reshape(columns, width_out)],
        "unpack",
        flops=2 * columns * columns * width_out,
        touched=1 << 20,
        scratch=[pltpu.VMEM((columns, columns), bf16)],
    )
    return advected, tendencies.reshape(cells_x, cells_y, width_out)


def solution(mesh):
    placed = (
        P("face", "blk", None),
        P("face", "blk", None),
        P("face", "blk", None),
        P("face", "blk"),
        P("face", "blk", None),
        P("face", "blk"),
        P("blk", None, None),
        P("blk", None, None, None),
        P("blk", None, None),
    )
    return jax.shard_map(
        local,
        mesh=mesh,
        in_specs=placed,
        out_specs=(P("face", "blk", None), P("face", "blk", None)),
        check_vma=False,
    )
```

```python
import jax
import jax.numpy as jnp
from jax import lax
from jax.experimental import pallas as pl
from jax.experimental.pallas import tpu as pltpu
from jax.sharding import PartitionSpec as P

SLOPE = 0.15
VMEM = pl.BlockSpec(memory_space=pltpu.VMEM)


HBM = pl.BlockSpec(memory_space=pltpu.HBM)


def call(kernel, outs, operands, name, flops=0, touched=0, scratch=(), specs=None, out_specs=None):
    return pl.pallas_call(
        kernel,
        out_shape=outs,
        in_specs=specs or [VMEM] * len(operands),
        out_specs=out_specs or jax.tree.map(lambda _: VMEM, outs),
        scratch_shapes=list(scratch),
        compiler_params=pltpu.CompilerParams(vmem_limit_bytes=16 << 20),
        cost_estimate=pl.CostEstimate(flops=flops, bytes_accessed=touched, transcendentals=0),
        name=name,
    )(*operands)


def in_hbm(array):
    return pltpu.with_memory_space_constraint(array, pltpu.HBM)


def edges_kernel(
    tracer,
    wind_x,
    wind_y,
    target,
    forcing,
    last_x,
    first_x,
    last_y,
    first_y,
    held_target,
    held_forcing,
    low_rows,
    high_rows,
    speed_x,
    speed_y,
    arrived,
):
    cells_x, cells_y, _ = tracer.shape
    copies = [
        pltpu.make_async_copy(source, target, arrived.at[index])
        for index, (source, target) in enumerate(
            (
                (tracer.at[pl.ds(cells_x - 1, 1)], last_x.at[pl.ds(0, 1)]),
                (tracer.at[pl.ds(0, 1)], first_x.at[pl.ds(0, 1)]),
                (wind_x.at[pl.ds(cells_x - 1, 1)], speed_x),
                (tracer.at[:, pl.ds(0, 8), :], low_rows),
                (tracer.at[:, pl.ds(cells_y - 8, 8), :], high_rows),
                (wind_y.at[:, pl.ds(cells_y - 16, 16), :], speed_y),
                (target, held_target),
                (forcing, held_forcing),
            )
        )
    ]
    for copy in copies:
        copy.start()
    first_x[1] = jnp.zeros(first_x.shape[1:], jnp.float32)
    first_y[1] = jnp.zeros(first_y.shape[1:], jnp.float32)
    for copy in copies:
        copy.wait()
    last_x[1] = speed_x[0].astype(jnp.float32)
    first_y[0] = low_rows[:, 0, :]
    last_y[0] = high_rows[:, 7, :]
    last_y[1] = speed_y[...].astype(jnp.float32)[:, 15, :]


def row_of(target, columns):
    cells_x, cells_y = target.shape
    lane = lax.broadcasted_iota(jnp.int32, (cells_y, columns), 1)
    place = lax.broadcasted_iota(jnp.int32, (cells_y, columns), 0)
    spread = jnp.where(lane % cells_y == place, 1.0, 0.0).astype(jnp.bfloat16)
    high = jnp.dot(
        (target >> 4).astype(jnp.float32).astype(jnp.bfloat16),
        spread,
        preferred_element_type=jnp.float32,
    )
    low = jnp.dot(
        (target & 15).astype(jnp.float32).astype(jnp.bfloat16),
        spread,
        preferred_element_type=jnp.float32,
    )
    lane = lax.broadcasted_iota(jnp.int32, (cells_x, columns), 1)
    place = lax.broadcasted_iota(jnp.int32, (cells_x, columns), 0)
    own = jnp.where(lane // cells_y == place, 16.0 * high + low, 0.0)
    return jnp.sum(own, axis=0, keepdims=True).astype(jnp.int32)


def fill_slots(target, to_slots):
    slots, columns = to_slots.shape
    step = 128
    row = row_of(target[...], columns)

    def body(index, _):
        chunk = pl.ds(pl.multiple_of(index * step, step), step)
        place = lax.broadcasted_iota(jnp.int32, (step, columns), 0) + index * step
        to_slots[chunk, :] = jnp.where(row == place, 1.0, 0.0).astype(jnp.bfloat16)
        return 0

    lax.fori_loop(0, slots // step, body, 0)


def fill_columns(target, to_columns, rows):
    cells_y = target.shape[1]
    turned = jnp.transpose(target[...].astype(jnp.float32)).astype(jnp.int32)
    place = lax.broadcasted_iota(jnp.int32, (cells_y, to_columns.shape[1]), 1)
    for start in range(rows.start, rows.stop, cells_y):
        i = start // cells_y
        to_columns[start : start + cells_y, :] = jnp.where(
            turned[:, i : i + 1] == place, 1.0, 0.0
        ).astype(jnp.bfloat16)


def select_kernel(target, forcing, to_slots, packed):
    @pl.when(lax.axis_index("face") % 2 == 1)
    def _():
        fill_slots(target, to_slots)
        packed[...] = jnp.dot(
            to_slots[...], forcing[...], preferred_element_type=jnp.float32
        ).astype(jnp.bfloat16)


def advect_kernel(
    tracer,
    wind_x,
    wind_y,
    area,
    west,
    east,
    south,
    north,
    to_slots,
    packed_forcing,
    target,
    forcing,
    advected,
    features,
    to_columns,
    rounded,
    own_slots,
):
    cells_x, cells_y, levels = tracer.shape
    second = lax.axis_index("face") % 2 == 0
    inverse = jnp.transpose(1.0 / area[...])
    place = lax.broadcasted_iota(jnp.int32, (cells_y, levels), 0)
    west_speed = west[1]
    flux_before = jnp.maximum(west_speed, 0.0) * west[0] + jnp.minimum(west_speed, 0.0) * tracer[0]
    for i in range(cells_x):
        here = tracer[i]
        after = tracer[i + 1] if i + 1 < cells_x else east[0]
        speed = wind_x[i].astype(jnp.float32)
        flux_x = jnp.maximum(speed, 0.0) * here + jnp.minimum(speed, 0.0) * after
        speed = wind_y[i].astype(jnp.float32)
        beyond = jnp.where(
            place == cells_y - 1, north[0, i : i + 1, :], pltpu.roll(here, cells_y - 1, 0)
        )
        flux_y = jnp.maximum(speed, 0.0) * here + jnp.minimum(speed, 0.0) * beyond
        south_speed = south[1, i : i + 1, :]
        south_flux = (
            jnp.maximum(south_speed, 0.0) * south[0, i : i + 1, :]
            + jnp.minimum(south_speed, 0.0) * here[0:1, :]
        )
        flux_y_before = jnp.where(place == 0, south_flux, pltpu.roll(flux_y, 1, 0))
        spread = (flux_x - flux_before) + (flux_y - flux_y_before)
        moved = here - spread * inverse[:, i : i + 1]
        advected[i] = moved
        rounded[i * cells_y : (i + 1) * cells_y, :] = moved.astype(jnp.bfloat16)
        flux_before = flux_x

    def put(part, values):
        features[:, part] = values.astype(jnp.bfloat16)

    @pl.when(jnp.logical_not(second))
    def _():
        features[:, levels:] = packed_forcing[...]
        put(
            slice(0, levels),
            jnp.dot(to_slots[...], rounded[...], preferred_element_type=jnp.float32),
        )

    @pl.when(second)
    def _():
        fill_columns(target, to_columns, slice(0, to_columns.shape[0]))
        fill_slots(target, own_slots)
        put(
            slice(0, levels),
            jnp.dot(own_slots[...], rounded[...], preferred_element_type=jnp.float32),
        )
        put(
            slice(levels, features.shape[1]),
            jnp.dot(own_slots[...], forcing[...], preferred_element_type=jnp.float32),
        )


def net_kernel(
    rows_in, w_in, w_hidden, w_out, advected, result, advected_out, ping, pong, stored
):
    step = 256
    copy = pltpu.make_async_copy(advected, advected_out, stored)
    copy.start()

    def leaky(values):
        return jnp.maximum(values, SLOPE * values)

    def layer(source, weights, target, finish):
        for start in range(0, source.shape[0], step):
            rows = slice(start, start + step)
            sums = jnp.dot(source[rows, :], weights, preferred_element_type=jnp.float32)
            target[rows, :] = finish(sums).astype(jnp.bfloat16)

    layer(rows_in, w_in[0], ping, leaky)
    here, there = ping, pong
    for index in range(w_hidden.shape[1]):
        layer(here, w_hidden[0, index], there, leaky)
        here, there = there, here
    layer(here, w_out[0], result, lambda sums: sums)
    copy.wait()


def unpack_kernel(target, to_columns, returned, tendencies, own_columns):
    columns = tendencies.shape[0]
    step = 256

    def take(one_hot, rows):
        tendencies[rows, :] = jnp.dot(
            one_hot[rows, :], returned[...], preferred_element_type=jnp.float32
        ).astype(jnp.bfloat16)

    @pl.when(lax.axis_index("face") % 2 == 0)
    def _():
        for start in range(0, columns, step):
            take(to_columns, slice(start, start + step))

    @pl.when(lax.axis_index("face") % 2 == 1)
    def _():
        for start in range(0, columns, step):
            rows = slice(start, start + step)
            fill_columns(target, own_columns, rows)
            take(own_columns, rows)


def neighbours(axis):
    count = lax.axis_size(axis)
    forward = [(i, (i + 1) % count) for i in range(count)]
    return forward, [(target, source) for source, target in forward]


def local(tracer, wind_x, wind_y, cell_area, forcing, group_map, w_in, w_hidden, w_out):
    groups = lax.axis_size("blk")
    cells_x, cells_y, levels = tracer.shape
    columns = cells_x * cells_y
    slots_per = columns // groups
    width = levels + forcing.shape[2]
    width_out = w_out.shape[2]
    f32, bf16 = jnp.float32, jnp.bfloat16
    shaped = pltpu.VMEM
    result_of = jax.ShapeDtypeStruct

    last_x, first_x, last_y, first_y, target, forcing = call(
        edges_kernel,
        [
            shaped((2, cells_y, levels), f32),
            shaped((2, cells_y, levels), f32),
            shaped((2, cells_x, levels), f32),
            shaped((2, cells_x, levels), f32),
            shaped(group_map.shape, group_map.dtype),
            shaped((columns, forcing.shape[2]), bf16),
        ],
        [
            in_hbm(array)
            for array in (tracer, wind_x, wind_y, group_map, forcing.reshape(columns, -1))
        ],
        "edges",
        touched=1 << 19,
        scratch=[
            pltpu.VMEM((cells_x, 8, levels), f32),
            pltpu.VMEM((cells_x, 8, levels), f32),
            pltpu.VMEM((1, cells_y, levels), bf16),
            pltpu.VMEM((cells_x, 16, levels), bf16),
            pltpu.SemaphoreType.DMA((8,)),
        ],
        specs=[HBM] * 5,
    )
    forward, backward = neighbours("face")
    west = lax.ppermute(last_x, "face", forward)
    east = lax.ppermute(first_x, "face", backward)
    forward, backward = neighbours("blk")
    south = lax.ppermute(last_y, "blk", forward)
    north = lax.ppermute(first_y, "blk", backward)

    to_slots, packed_forcing = call(
        select_kernel,
        [shaped((columns, columns), bf16), shaped(forcing.shape, bf16)],
        [target, forcing],
        "select",
        flops=2 * columns * forcing.size,
        touched=4 << 20,
    )
    advected, features, to_columns = call(
        advect_kernel,
        [
            shaped(tracer.shape, f32),
            shaped((columns, width), bf16),
            shaped((columns, columns), bf16),
        ],
        [
            tracer,
            wind_x,
            wind_y,
            cell_area,
            west,
            east,
            south,
            north,
            to_slots,
            packed_forcing,
            target,
            forcing,
        ],
        "advect",
        flops=2 * columns * columns * levels,
        touched=6 << 20,
        scratch=[
            pltpu.VMEM((columns, levels), bf16),
            pltpu.VMEM((columns, columns), bf16),
        ],
    )
    received = lax.all_to_all(
        features.reshape(groups, slots_per, width), "blk", split_axis=0, concat_axis=0, tiled=True
    )
    result, advected = call(
        net_kernel,
        [shaped((columns, width_out), bf16), result_of(tracer.shape, f32)],
        [received.reshape(columns, width), w_in, w_hidden, w_out, advected],
        "net",
        flops=2 * columns * (w_in.size + w_hidden.size + w_out.size),
        touched=5 << 20,
        scratch=[pltpu.VMEM((columns, w_in.shape[2]), bf16)] * 2 + [pltpu.SemaphoreType.DMA],
        out_specs=[VMEM, HBM],
    )
    returned = lax.all_to_all(
        result.reshape(groups, slots_per, width_out), "blk", split_axis=0, concat_axis=0, tiled=True
    )
    tendencies = call(
        unpack_kernel,
        result_of((columns, width_out), bf16),
        [target, to_columns, returned.reshape(columns, width_out)],
        "unpack",
        flops=2 * columns * columns * width_out,
        touched=1 << 20,
        scratch=[pltpu.VMEM((columns, columns), bf16)],
    )
    return advected, tendencies.reshape(cells_x, cells_y, width_out)


def solution(mesh):
    placed = (
        P("face", "blk", None),
        P("face", "blk", None),
        P("face", "blk", None),
        P("face", "blk"),
        P("face", "blk", None),
        P("face", "blk"),
        P("blk", None, None),
        P("blk", None, None, None),
        P("blk", None, None),
    )
    return jax.shard_map(
        local,
        mesh=mesh,
        in_specs=placed,
        out_specs=(P("face", "blk", None), P("face", "blk", None)),
        check_vma=False,
    )
```
